256 devices in a mesh: wide: 64 (over z, x, y_hi), narrow: 4 (over y_lo, core).
Axes of the slice: x: 4, y: 4 (y_hi: 2, y_lo: 2; y = y_hi * 2 + y_lo), z: 8, core: 2. Of those that a mesh axis runs over, the one named last changes fastest.
Arguments:
- residual: bfloat16 [512, 8192], P('wide'), may hold values from -400 to 400
- norm_gain: float32 [8192], P('narrow'), may hold values from 0.1 to 1.9
- gate_weight: bfloat16 [8192, 32768], P('narrow', 'wide'), may hold values from -0.0625 to 0.0625
- up_weight: bfloat16 [8192, 32768], P('narrow', 'wide'), may hold values from -0.0625 to 0.0625
- down_weight: bfloat16 [32768, 8192], P('wide', 'narrow'), may hold values from -0.03125 to 0.03125
- out_weight: bfloat16 [8192, 8192], P('wide', 'narrow'), may hold values from -0.0625 to 0.0625
- queries: bfloat16 [512, 8192], P(('wide', 'narrow')), may hold values from -64 to 64
- key_fresh: bfloat16 [512, 256], P(('wide', 'narrow')), may hold values from -4 to 4
- value_fresh: bfloat16 [512, 256], P(('wide', 'narrow')), may hold values from -4 to 4
- key_cache: bfloat16 [512, 2048, 256], P(('wide', 'narrow')), may hold values from -4 to 4
- value_cache: bfloat16 [512, 2048, 256], P(('wide', 'narrow')), may hold values from -4 to 4
- lengths: int32 [512], P(('wide', 'narrow')), may hold values from 1 to 2048, 524288 in all
Outputs:
- branch: bfloat16 [512, 8192], P('wide', 'narrow')
The draws below stay inside these ranges and needn't reach their ends.
Inputs may be any that keep to these rules, and one draw needn't show every extreme that they name: Slots 0 to lengths - 1 of a sequence's cache are its earlier tokens; the new token follows them.
All inputs are finite; a program needn't handle non-finite values. No bound on the sum of `lengths` on one device may be relied on, other than what follows from the above.
Results may differ from the reference program's by a relative error of at most 0.022.
Values may be sent and summed in bfloat16 or wider, within the bound.
A program may use at most 64 MiB of HBM per device.

```python
import math
import jax
import jax.numpy as jnp
import numpy as np
from jax import lax

D = 8192
FF = 32768
HEADS = 32
HEAD_DIM = 256
CACHE = 2048
BATCH = 512
FEAT_BLOCK = 2048
N_NARROW = 4


def bounded_normal(key, shape):
    return jnp.clip(jax.random.normal(key, shape, jnp.float32), -4.0, 4.0)


def draw_queries(key, part):
    key = jax.random.fold_in(key, 1)
    values = bounded_normal(key, (BATCH, HEADS, HEAD_DIM))
    return values.reshape(BATCH, HEADS * HEAD_DIM).astype(jnp.bfloat16)


def draw_key_cache(key, part):
    key = jax.random.fold_in(key, 2)
    values = bounded_normal(key, (BATCH, CACHE, HEAD_DIM))
    return values.astype(jnp.bfloat16)


def draw_key_fresh(key, part):
    key = jax.random.fold_in(key, 3)
    values = bounded_normal(key, (BATCH, HEAD_DIM))
    return values.astype(jnp.bfloat16)


def draw_residual(key, part):
    key = jax.random.fold_in(key, 4)
    row_scale = jnp.exp(jax.random.uniform(jax.random.fold_in(key, 1), (BATCH, 1), jnp.float32, 0.0, math.log(10.0)))
    col_scale = jnp.exp(jax.random.uniform(jax.random.fold_in(key, 2), (1, D), jnp.float32, 0.0, math.log(10.0)))
    values = bounded_normal(jax.random.fold_in(key, 5), (BATCH, D))
    return (values * row_scale * col_scale).astype(jnp.bfloat16)


def level_of(rng, dims, pieces, least, largest):
    gain = 1.0
    for axis_at, parts in pieces:
        steps = jax.random.uniform(jax.random.fold_in(jax.random.fold_in(rng, 6), axis_at), (parts,), jnp.float32, least / len(pieces), largest / len(pieces))
        gain = gain * jnp.repeat(jnp.exp(steps), dims[axis_at] // parts).reshape((-1,) + (1,) * (len(dims) - 1 - axis_at))
    return gain


def length_profile(number_of, total, most, skew):
    portions = [(1 << 20) // math.isqrt(standing ** skew) + 1 for standing in range(2, number_of + 1)]
    surplus, given = total - most - (number_of - 1), [1] * (number_of - 1)
    while surplus > 0:
        movable = [i for i in range(number_of - 1) if given[i] < most]
        pool, remaining = sum([portions[i] for i in movable]), surplus
        for i in movable:
            addition = min(most - given[i], max(1, remaining * portions[i] // pool), surplus)
            given[i] = given[i] + addition
            surplus = surplus - addition
    return np.array([most] + given)


def ragged(rng, count, total, reach, slope):
    if count == 2:
        one = jax.random.randint(rng, (), max(1, total - reach), min(reach, total - 1) + 1)
        return jnp.stack([one, total - one])
    sizes = jnp.asarray(length_profile(count, total, reach, slope), jnp.int32)
    couples = (count - 1) // 2
    source_of, taker = sizes[1:1 + 2 * couples:2], sizes[2:2 + 2 * couples:2]
    slack = jnp.minimum(source_of - 1, reach - taker)
    shifted = jax.random.randint(jax.random.fold_in(rng, 1), (couples,), 0, 1 << 20) % (slack + 1)
    sizes = sizes.at[1:1 + 2 * couples:2].set(source_of - shifted).at[2:2 + 2 * couples:2].set(taker + shifted)
    return sizes[jax.random.permutation(jax.random.fold_in(rng, 2), count)]


def scatter_about(own_key, shape, width, reach, shards=(), dtype=jnp.bfloat16):
    drawn = jax.random.normal(own_key, shape, jnp.float32) * width
    if len(shards) > 0:
        drawn = level_of(own_key, shape, shards, -0.22, 0.18) * drawn
    return jnp.clip(drawn, min=-reach, max=reach).astype(dtype)


def setup_inputs(seed: int = 0) -> dict:
    key_of = jax.random.split(jax.random.key(seed), 13)
    residual = draw_residual(jax.random.fold_in(key_of[12], 71), 0)
    norm_gain = jnp.clip(1.0 + 0.18 * jax.random.normal(key_of[1], (D,), jnp.float32), 0.1, 1.9)
    gate_weight = scatter_about(key_of[2], (D, FF), D ** -0.5, 0.0625, ((0, 4), (1, 64)))
    up_weight = scatter_about(key_of[3], (D, FF), D ** -0.5, 0.0625, ((0, 4), (1, 64)))
    down_weight = scatter_about(key_of[4], (FF, D), FF ** -0.5, 0.03125, ((0, 64), (1, 4)))
    out_weight = scatter_about(key_of[5], (HEADS * HEAD_DIM, D), (HEADS * HEAD_DIM) ** -0.5, 0.0625, ((0, 64), (1, 4)))
    queries = draw_queries(jax.random.fold_in(key_of[12], 71), 0)
    key_fresh = draw_key_fresh(jax.random.fold_in(key_of[12], 71), 0)
    value_fresh = scatter_about(key_of[8], (BATCH, HEAD_DIM), 1.0, 4.0, ((0, 256),))
    key_cache = draw_key_cache(jax.random.fold_in(key_of[12], 71), 0)
    value_cache = scatter_about(key_of[10], (BATCH, CACHE, HEAD_DIM), 1.0, 4.0, ((0, 256),))
    lengths = ragged(key_of[11], BATCH, BATCH * CACHE // 2, CACHE, 2).astype(jnp.int32)
    return {"residual": residual, "norm_gain": norm_gain, "gate_weight": gate_weight, "up_weight": up_weight, "down_weight": down_weight, "out_weight": out_weight, "queries": queries, "key_fresh": key_fresh, "value_fresh": value_fresh, "key_cache": key_cache, "value_cache": value_cache, "lengths": lengths}


epsilon = 1e-05
masked_score = -1e+30

def one_sequence(items):
    query_row, key_new_row, value_new_row, key_rows, value_rows, length = items
    scale = 1.0 / math.sqrt(HEAD_DIM)
    query_heads = query_row.reshape(HEADS, HEAD_DIM).astype(jnp.float32)
    scores = jnp.dot(query_heads, key_rows.astype(jnp.float32).T, precision=lax.Precision.HIGHEST) * scale
    fresh = jnp.dot(query_heads, key_new_row.astype(jnp.float32), precision=lax.Precision.HIGHEST) * scale
    included = jnp.arange(CACHE) < length
    masked = jnp.where(included[None, :], scores, masked_score)
    peak = jnp.maximum(lax.optimization_barrier(jnp.max(masked, axis=1)), fresh)
    weights = jnp.exp(masked - peak[:, None]).astype(jnp.bfloat16)
    fresh_weight = jnp.exp(fresh - peak).astype(jnp.bfloat16)
    total = lax.optimization_barrier(jnp.sum(weights.astype(jnp.float32), axis=1)) + fresh_weight.astype(jnp.float32)
    mixed = jnp.dot(weights.astype(jnp.float32), value_rows.astype(jnp.float32), precision=lax.Precision.HIGHEST)
    mixed = mixed + fresh_weight.astype(jnp.float32)[:, None] * value_new_row.astype(jnp.float32)[None, :]
    return (mixed / total[:, None]).astype(jnp.bfloat16).reshape(HEADS * HEAD_DIM)

def reference(residual, norm_gain, gate_weight, up_weight, down_weight, out_weight, queries, key_fresh, value_fresh, key_cache, value_cache, lengths):
    stream = residual.astype(jnp.float32)
    row_mean = lax.optimization_barrier(jnp.mean(stream, axis=1, keepdims=True))
    centered = stream - row_mean
    row_var = lax.optimization_barrier(jnp.mean(centered * centered, axis=1, keepdims=True))
    normed = (centered * lax.rsqrt(row_var + epsilon) * norm_gain).astype(jnp.bfloat16)
    gate_sum = jnp.zeros((BATCH, FF), jnp.float32)
    up_sum = jnp.zeros((BATCH, FF), jnp.float32)
    for block_index in range(N_NARROW):
        lower = block_index * FEAT_BLOCK
        upper = lower + FEAT_BLOCK
        feature_cols = normed[:, lower:upper]
        gate_part = lax.optimization_barrier(jnp.dot(feature_cols, gate_weight[lower:upper], preferred_element_type=jnp.float32).astype(jnp.bfloat16))
        up_part = lax.optimization_barrier(jnp.dot(feature_cols, up_weight[lower:upper], preferred_element_type=jnp.float32).astype(jnp.bfloat16))
        gate_sum = gate_sum + gate_part.astype(jnp.float32)
        up_sum = up_sum + up_part.astype(jnp.float32)
    hidden = (jax.nn.silu(gate_sum) * up_sum).astype(jnp.bfloat16)
    heads = lax.map(one_sequence, (queries, key_fresh, value_fresh, key_cache, value_cache, lengths))
    attention_proj = jnp.dot(heads, out_weight, preferred_element_type=jnp.float32)
    feedforward = jnp.dot(hidden, down_weight, preferred_element_type=jnp.float32)
    return (attention_proj + feedforward).astype(jnp.bfloat16)
```

```python
import math

import jax
import jax.numpy as jnp
from jax import lax
from jax.experimental import pallas as pl
from jax.experimental.pallas import tpu as pltpu
from jax.sharding import PartitionSpec as P

HEADS = 32
HEAD_DIM = 256
NZ, NX = 8, 4
ROWS = 8
COLS = 2048
HID = 512

epsilon = 1e-05
masked_score = -1e30
F32 = jnp.float32
BF16 = jnp.bfloat16


def kernel(
    residual,
    norm_gain,
    gate_weight,
    up_weight,
    down_weight,
    out_weight,
    queries,
    key_fresh,
    value_fresh,
    key_cache,
    value_cache,
    lengths,
    out,
    v_res,
    v_gain,
    v_gate,
    v_up,
    v_down,
    v_outw,
    v_q,
    v_kf,
    v_vf,
    v_kc,
    v_vc,
    qh,
    xb,
    part,
    part_in,
    pair,
    pair_in,
    hid,
    hn,
    ht,
    hs,
    hz,
    hx,
    hf,
    po,
    relay,
    direct,
    merged,
    zs,
    zr,
    fin,
    fin_in,
    local_sem,
    send_sem,
    recv_sem,
):
    wide, narrow = lax.axis_index("wide"), lax.axis_index("narrow")
    z, x, yh = wide // 8, (wide // 2) % 4, wide % 2
    yl, c = narrow // 2, narrow % 2

    def at(z_, x_, yh_, n_):
        return ((z_ * 4 + x_) * 2 + yh_, n_)

    def z_peer(d):
        return at((z + d) % 8, x, yh, narrow)

    def x_peer(d):
        return at(z, (x + d) % 4, yh, narrow)

    y_peer = at(z, x, 1 - yh, narrow)

    def n_peer(d):
        return at(z, x, yh, (narrow + d) % 4)

    core_peer = at(z, x, yh, yl * 2 + 1 - c)
    pair_peer = at(z, x, yh, (1 - yl) * 2 + c)

    names = [
        (residual, v_res),
        (norm_gain, v_gain),
        (queries, v_q),
        (key_fresh, v_kf),
        (value_fresh, v_vf),
        (key_cache, v_kc),
        (value_cache, v_vc),
        (gate_weight, v_gate),
        (up_weight, v_up),
        (out_weight, v_outw),
        (down_weight, v_down),
    ]
    loads = [
        pltpu.make_async_copy(src, dst, local_sem.at[i]) for i, (src, dst) in enumerate(names)
    ]
    for load in loads:
        load.start()
    (l_res, l_gain, l_q, l_kf, l_vf, l_kc, l_vc, l_gate, l_up, l_outw, l_down) = loads

    peers = (
        [z_peer(d) for d in range(1, 8)]
        + [x_peer(d) for d in range(1, 4)]
        + [y_peer]
        + [n_peer(d) for d in range(1, 4)]
    )
    barrier = pltpu.get_barrier_semaphore()
    for peer in peers:
        pl.semaphore_signal(barrier, inc=1, device_id=peer, device_id_type=pl.DeviceIdType.MESH)

    started = []

    def send(src, dst, peer):
        k = len(started)
        copy = pltpu.make_async_remote_copy(
            src_ref=src,
            dst_ref=dst,
            send_sem=send_sem.at[k],
            recv_sem=recv_sem.at[k],
            device_id=peer,
            device_id_type=pl.DeviceIdType.MESH,
        )
        copy.start()
        started.append(copy)
        return copy

    l_res.wait()
    l_gain.wait()
    stream = v_res[...].astype(F32)
    row_mean = jnp.mean(stream, axis=1, keepdims=True)
    centered = stream - row_mean
    row_var = jnp.mean(centered * centered, axis=1, keepdims=True)
    own = v_res[:, pl.ds(pl.multiple_of(narrow * COLS, COLS), COLS)].astype(F32) - row_mean
    normed = own * lax.rsqrt(row_var + epsilon) * v_gain[...]
    xb[0, x, z] = normed.astype(BF16)

    pl.semaphore_wait(barrier, len(peers))

    def gather_z(h):
        return [send(xb.at[h, x, z], xb.at[h, x, z], z_peer(d)) for d in (4, 3, 5, 2, 6, 1, 7)]

    swap = send(xb.at[0, x, z], xb.at[1, x, z], y_peer)
    gz0 = gather_z(0)

    l_q.wait()
    for b in range(2):
        for head in range(HEADS):
            qh[b, head : head + 1, :] = v_q[b : b + 1, head * HEAD_DIM : (head + 1) * HEAD_DIM].astype(F32)
    l_kf.wait()
    l_vf.wait()
    scale = 1.0 / math.sqrt(HEAD_DIM)
    l_kc.wait()
    l_vc.wait()
    for b in range(2):
        query = qh[b]
        scores = (
            lax.dot_general(
                query.astype(BF16), v_kc[b], (((1,), (1,)), ((), ())), preferred_element_type=F32
            )
            * scale
        )
        fresh = jnp.sum(query * v_kf[b : b + 1, :].astype(F32), axis=1, keepdims=True) * scale
        position = lax.broadcasted_iota(jnp.int32, scores.shape, 1)
        masked = jnp.where(position < lengths[b], scores, masked_score)
        peak = jnp.maximum(jnp.max(masked, axis=1, keepdims=True), fresh)
        weights = jnp.exp(masked - peak).astype(BF16)
        fresh_weight = jnp.exp(fresh - peak).astype(BF16).astype(F32)
        total = jnp.sum(weights.astype(F32), axis=1, keepdims=True) + fresh_weight
        mixed = jnp.dot(weights, v_vc[b], preferred_element_type=F32)
        mixed = mixed + fresh_weight * v_vf[b : b + 1, :].astype(F32)
        hn[narrow, b] = (mixed / total).astype(BF16)
    head_n = [send(hn.at[narrow], hn.at[narrow], n_peer(d)) for d in range(1, 4)]

    xm, xp = (x + 3) % 4, (x + 1) % 4
    xo = (x + 2) % 4

    def gather_x(h):
        lo = send(xb.at[h, x, 0:4], xb.at[h, x, 0:4], x_peer(1))
        hi = send(xb.at[h, x, 4:8], xb.at[h, x, 4:8], x_peer(3))
        lo2 = send(xb.at[h, x, 4:8], xb.at[h, x, 4:8], x_peer(1))
        hi2 = send(xb.at[h, x, 0:4], xb.at[h, x, 0:4], x_peer(3))
        return lo, hi, lo2, hi2

    def forward_x(h, copies):
        lo, hi, lo2, hi2 = copies
        lo.wait_recv()
        on_lo = send(xb.at[h, xm, 0:4], xb.at[h, xm, 0:4], x_peer(1))
        hi.wait_recv()
        on_hi = send(xb.at[h, xp, 4:8], xb.at[h, xp, 4:8], x_peer(3))
        return lo2, hi2, on_lo, on_hi

    def arrive(copies):
        for copy in copies:
            copy.wait_recv()

    arrive(gz0)
    gx0 = gather_x(0)
    swap.wait_recv()
    gz1 = gather_z(1)

    arrive(head_n)
    for n in range(4):
        for b in range(2):
            rows = hn[n, b].astype(F32)
            ht[0, :, n * 2 + b, :] = rows[:, :128]
            ht[1, :, n * 2 + b, :] = rows[:, 128:]
    for half in range(2):
        hs[:, :, half] = ht[half].reshape(NZ, NX, 8, 128).astype(BF16)
    hz[:, z] = hs[z]
    head_z = [
        send(hs.at[(z + d) % 8], hz.at[:, z], z_peer(d)) for d in (4, 3, 5, 2, 6, 1, 7)
    ]
    gx0 = forward_x(0, gx0)
    arrive(head_z)
    hx[x] = hz[x]
    head_x = [send(hz.at[(x + d) % 4], hx.at[x], x_peer(d)) for d in (2, 1, 3)]
    arrive(gz1)
    gx1 = gather_x(1)
    arrive(gx0)

    l_gate.wait()
    l_up.wait()

    def gate_up(h):
        def body(j, _):
            cols = pl.ds(pl.multiple_of(j * 256, 256), 256)
            rows = xb[h].reshape(256, COLS)
            gate = jnp.dot(rows, v_gate[:, cols], preferred_element_type=F32).astype(BF16)
            part[h, 0, 0, :, cols] = gate[:128]
            part[h, 1, 0, :, cols] = gate[128:]
            up = jnp.dot(rows, v_up[:, cols], preferred_element_type=F32).astype(BF16)
            part[h, 0, 1, :, cols] = up[:128]
            part[h, 1, 1, :, cols] = up[128:]
            return 0

        lax.fori_loop(0, 2, body, 0)
        return send(part.at[h, 1 - c], part_in.at[h], core_peer)

    def pair_sum(h, copy):
        copy.wait_recv()
        pair[h] = (part[h, c].astype(F32) + part_in[h].astype(F32)).astype(BF16)
        return send(pair.at[h], pair_in.at[h], pair_peer)

    def make_hidden(h, copy):
        copy.wait_recv()
        gate = pair[h, 0].astype(F32) + pair_in[h, 0].astype(F32)
        up = pair[h, 1].astype(F32) + pair_in[h, 1].astype(F32)
        hid[h, c] = (gate / (1.0 + jnp.exp(-gate)) * up).astype(BF16)
        return send(hid.at[h, c], hid.at[h, c], core_peer)

    def project(h, copy, heads):
        copy.wait_recv()

        def body(j, _):
            cols = pl.ds(pl.multiple_of(j * 512, 512), 512)
            acc = jnp.dot(hid[h].reshape(256, HID), v_down[:, cols], preferred_element_type=F32)
            acc = acc + jnp.dot(heads(), v_outw[:, cols], preferred_element_type=F32)
            po[h, :, :, :, cols] = acc.astype(BF16).reshape(NX, NZ, ROWS, 512)
            return 0

        lax.fori_loop(0, 4, body, 0)

    def scatter_x(h):
        r_lo = send(po.at[h, xo, 0:4], relay.at[h, 0], x_peer(1))
        r_hi = send(po.at[h, xo, 4:8], relay.at[h, 1], x_peer(3))
        d_hi = send(po.at[h, xp, 4:8], direct.at[h, 0], x_peer(1))
        d_lo = send(po.at[h, xm, 0:4], direct.at[h, 1], x_peer(3))
        return r_lo, r_hi, d_hi, d_lo

    def relay_x(h, copies):
        r_lo, r_hi, d_hi, d_lo = copies
        r_lo.wait_recv()
        po[h, xp, 0:4] = (po[h, xp, 0:4].astype(F32) + relay[h, 0].astype(F32)).astype(BF16)
        m_lo = send(po.at[h, xp, 0:4], merged.at[h, 0], x_peer(1))
        r_hi.wait_recv()
        po[h, xm, 4:8] = (po[h, xm, 4:8].astype(F32) + relay[h, 1].astype(F32)).astype(BF16)
        m_hi = send(po.at[h, xm, 4:8], merged.at[h, 1], x_peer(3))
        return d_hi, d_lo, m_lo, m_hi

    def scatter_z(h, copies):
        arrive(copies)
        zs[h, 0:4] = (
            po[h, x, 0:4].astype(F32) + merged[h, 0].astype(F32) + direct[h, 1].astype(F32)
        ).astype(BF16)
        zs[h, 4:8] = (
            po[h, x, 4:8].astype(F32) + merged[h, 1].astype(F32) + direct[h, 0].astype(F32)
        ).astype(BF16)
        return [
            send(zs.at[h, (z + d) % 8], zr.at[h, z], z_peer(d)) for d in (4, 3, 5, 2, 6, 1, 7)
        ]

    def finish(h, copies):
        arrive(copies)
        acc = zs[h, z].astype(F32)
        for d in range(1, 8):
            acc = acc + zr[h, (z + d) % 8].astype(F32)
        return acc

    co0 = gate_up(0)
    arrive(head_x)
    head_y = send(hx.at[:, :, 1 - yh], hf, y_peer)
    gx1 = forward_x(1, gx1)
    pa0 = pair_sum(0, co0)
    arrive(gx1)
    co1 = gate_up(1)
    hi0 = make_hidden(0, pa0)
    pa1 = pair_sum(1, co1)
    head_y.wait_recv()
    l_outw.wait()
    l_down.wait()
    project(0, hi0, lambda: hx[:, :, yh].reshape(256, 128))
    sx0 = scatter_x(0)
    sx0 = relay_x(0, sx0)
    hi1 = make_hidden(1, pa1)
    project(1, hi1, lambda: hf[...].reshape(256, 128))
    sx1 = scatter_x(1)
    sz0 = scatter_z(0, sx0)
    sx1 = relay_x(1, sx1)
    own_half = finish(0, sz0)
    sz1 = scatter_z(1, sx1)
    fin[...] = finish(1, sz1).astype(BF16)
    last = send(fin, fin_in, y_peer)
    last.wait_recv()
    out[...] = (own_half + fin_in[...].astype(F32)).astype(BF16)

    for copy in started:
        copy.wait_send()


SENDS = 74


def local(*args):
    args = list(args)
    args[1] = args[1].reshape(1, COLS)
    anywhere = pl.BlockSpec(memory_space=pl.ANY)
    vm = pltpu.VMEM
    return pl.pallas_call(
        kernel,
        out_shape=jax.ShapeDtypeStruct((ROWS, COLS), BF16),
        in_specs=[anywhere] * 11 + [pl.BlockSpec(memory_space=pltpu.SMEM)],
        out_specs=pl.BlockSpec(memory_space=pltpu.VMEM),
        scratch_shapes=[
            vm((8, 8192), BF16),
            vm((1, COLS), F32),
            vm((2048, HID), BF16),
            vm((2048, HID), BF16),
            vm((HID, COLS), BF16),
            vm((128, COLS), BF16),
            vm((2, 8192), BF16),
            vm((2, HEAD_DIM), BF16),
            vm((2, HEAD_DIM), BF16),
            vm((2, 2048, HEAD_DIM), BF16),
            vm((2, 2048, HEAD_DIM), BF16),
            vm((2, HEADS, HEAD_DIM), F32),
            vm((2, NX, NZ, ROWS, COLS), BF16),
            vm((2, 2, 2, 128, HID), BF16),
            vm((2, 2, 128, HID), BF16),
            vm((2, 2, 128, HID), BF16),
            vm((2, 2, 128, HID), BF16),
            vm((2, 2, 128, HID), BF16),
            vm((4, 2, HEADS, HEAD_DIM), BF16),
            vm((2, HEADS, 8, 128), F32),
            vm((NZ, NX, 2, 8, 128), BF16),
            vm((NX, NZ, 2, 8, 128), BF16),
            vm((NX, NZ, 2, 8, 128), BF16),
            vm((NX, NZ, 8, 128), BF16),
            vm((2, NX, NZ, ROWS, COLS), BF16),
            vm((2, 2, 4, ROWS, COLS), BF16),
            vm((2, 2, 4, ROWS, COLS), BF16),
            vm((2, 2, 4, ROWS, COLS), BF16),
            vm((2, NZ, ROWS, COLS), BF16),
            vm((2, NZ, ROWS, COLS), BF16),
            vm((ROWS, COLS), BF16),
            vm((ROWS, COLS), BF16),
            pltpu.SemaphoreType.DMA((11,)),
            pltpu.SemaphoreType.DMA((SENDS,)),
            pltpu.SemaphoreType.DMA((SENDS,)),
        ],
        compiler_params=pltpu.CompilerParams(
            collective_id=0, has_side_effects=True, vmem_limit_bytes=56 * 1024 * 1024
        ),
    )(*args)


def solution(mesh):
    return jax.shard_map(
        local,
        mesh=mesh,
        in_specs=(
            P("wide", None),
            P("narrow"),
            P("narrow", "wide"),
            P("narrow", "wide"),
            P("wide", "narrow"),
            P("wide", "narrow"),
            P(("wide", "narrow"), None),
            P(("wide", "narrow"), None),
            P(("wide", "narrow"), None),
            P(("wide", "narrow"), None, None),
            P(("wide", "narrow"), None, None),
            P(("wide", "narrow")),
        ),
        out_specs=P("wide", "narrow"),
        check_vma=False,
    )
```

```python
import math

import jax
import jax.numpy as jnp
from jax import lax
from jax.experimental import pallas as pl
from jax.experimental.pallas import tpu as pltpu
from jax.sharding import PartitionSpec as P

HEADS = 32
HEAD_DIM = 256
NZ, NX = 8, 4
ROWS = 8
COLS = 2048
HID = 512
SLOTS = (0, 1, 7, 2, 6, 3, 5, 4)

epsilon = 1e-05
masked_score = -1e30
F32 = jnp.float32
BF16 = jnp.bfloat16


def kernel(
    residual,
    norm_gain,
    gate_weight,
    up_weight,
    down_weight,
    out_weight,
    queries,
    key_fresh,
    value_fresh,
    key_cache,
    value_cache,
    lengths,
    out,
    v_res,
    v_gain,
    v_gate,
    v_up,
    v_down,
    v_outw,
    v_q,
    v_kf,
    v_vf,
    v_kc,
    v_vc,
    qh,
    xb,
    part,
    part_in,
    pair,
    pair_in,
    hid,
    hn,
    ht,
    hs,
    hz,
    hx,
    hf,
    po,
    relay,
    direct,
    merged,
    zs,
    zr,
    fin,
    fin_in,
    local_sem,
    send_sem,
    recv_sem,
):
    wide, narrow = lax.axis_index("wide"), lax.axis_index("narrow")
    z, x, yh = wide // 8, (wide // 2) % 4, wide % 2
    yl, c = narrow // 2, narrow % 2

    def at(z_, x_, yh_, n_):
        return ((z_ * 4 + x_) * 2 + yh_, n_)

    def z_peer(d):
        return at((z + d) % 8, x, yh, narrow)

    def x_peer(d):
        return at(z, (x + d) % 4, yh, narrow)

    y_peer = at(z, x, 1 - yh, narrow)

    def zy_peer(d):
        return at((z + d) % 8, x, 1 - yh, narrow)

    def n_peer(d):
        return at(z, x, yh, (narrow + d) % 4)

    core_peer = at(z, x, yh, yl * 2 + 1 - c)
    pair_peer = at(z, x, yh, (1 - yl) * 2 + c)

    names = [
        (residual, v_res),
        (norm_gain, v_gain),
        (queries, v_q),
        (key_fresh, v_kf),
        (value_fresh, v_vf),
        (key_cache, v_kc),
        (value_cache, v_vc),
        (gate_weight, v_gate),
        (up_weight, v_up),
        (out_weight, v_outw),
        (down_weight, v_down),
    ]
    loads = [
        pltpu.make_async_copy(src, dst, local_sem.at[i]) for i, (src, dst) in enumerate(names)
    ]
    (l_res, l_gain, l_q, l_kf, l_vf, l_kc, l_vc, l_gate, l_up, l_outw, l_down) = loads
    l_res.start()
    l_gain.start()

    peers = (
        [z_peer(d) for d in range(1, 8)]
        + [x_peer(d) for d in range(1, 4)]
        + [y_peer]
        + [zy_peer(d) for d in (1, 7, 2, 6)]
        + [n_peer(d) for d in range(1, 4)]
    )
    barrier = pltpu.get_barrier_semaphore()
    for peer in peers:
        pl.semaphore_signal(barrier, inc=1, device_id=peer, device_id_type=pl.DeviceIdType.MESH)

    started = []

    def send(src, dst, peer):
        k = len(started)
        copy = pltpu.make_async_remote_copy(
            src_ref=src,
            dst_ref=dst,
            send_sem=send_sem.at[k],
            recv_sem=recv_sem.at[k],
            device_id=peer,
            device_id_type=pl.DeviceIdType.MESH,
        )
        copy.start()
        started.append(copy)
        return copy

    got = {}
    waited = set()

    def arrive(*keys):
        for key in keys:
            if key in got and key not in waited:
                got[key].wait_recv()
                waited.add(key)

    l_res.wait()
    l_gain.wait()
    for load in loads[2:]:
        load.start()
    stream = v_res[...].astype(F32)
    row_mean = jnp.mean(stream, axis=1, keepdims=True)
    centered = stream - row_mean
    row_var = jnp.mean(centered * centered, axis=1, keepdims=True)
    own = v_res[:, pl.ds(pl.multiple_of(narrow * COLS, COLS), COLS)].astype(F32) - row_mean
    normed = own * lax.rsqrt(row_var + epsilon) * v_gain[...]
    xb[0, 0, 0, 0] = normed.astype(BF16)

    pl.semaphore_wait(barrier, len(peers))

    def swap():
        got["swap"] = send(xb.at[0, 0, 0, 0], xb.at[1, 0, 0, 0], y_peer)

    def gather_z(h, b):
        if h == 1 and b == 1:
            arrive("swap")
        straight = h == 1 and b == 0
        for j in range(4):
            d = SLOTS[b * 4 + j]
            if d:
                got["z", h, b, j] = send(
                    xb.at[0 if straight else h, 0, 0, 0],
                    xb.at[h, b, 0, j],
                    zy_peer(d) if straight else z_peer(d),
                )

    scale = 1.0 / math.sqrt(HEAD_DIM)

    def attend(b):
        for head in range(HEADS):
            qh[b, head : head + 1, :] = v_q[b : b + 1, head * HEAD_DIM : (head + 1) * HEAD_DIM].astype(F32)
        query = qh[b]
        scores = (
            lax.dot_general(
                query.astype(BF16), v_kc[b], (((1,), (1,)), ((), ())), preferred_element_type=F32
            )
            * scale
        )
        fresh = jnp.sum(query * v_kf[b : b + 1, :].astype(F32), axis=1, keepdims=True) * scale
        position = lax.broadcasted_iota(jnp.int32, scores.shape, 1)
        masked = jnp.where(position < lengths[b], scores, masked_score)
        peak = jnp.maximum(jnp.max(masked, axis=1, keepdims=True), fresh)
        weights = jnp.exp(masked - peak).astype(BF16)
        fresh_weight = jnp.exp(fresh - peak).astype(BF16).astype(F32)
        total = jnp.sum(weights.astype(F32), axis=1, keepdims=True) + fresh_weight
        mixed = jnp.dot(weights, v_vc[b], preferred_element_type=F32)
        mixed = mixed + fresh_weight * v_vf[b : b + 1, :].astype(F32)
        hn[narrow, b] = (mixed / total).astype(BF16)

    def gather_lo(h, b):
        if h == 1 and b == 0:
            arrive("swap")
        arrive(("z", h, b, 0), ("z", h, b, 1))
        got["lo", h, b] = send(xb.at[h, b, 0, 0:2], xb.at[h, b, 1, 0:2], x_peer(1))
        got["hi2", h, b] = send(xb.at[h, b, 0, 0:2], xb.at[h, b, 3, 0:2], x_peer(3))

    def gather_hi(h, b):
        arrive(("z", h, b, 2), ("z", h, b, 3))
        got["hi", h, b] = send(xb.at[h, b, 0, 2:4], xb.at[h, b, 3, 2:4], x_peer(3))
        got["lo2", h, b] = send(xb.at[h, b, 0, 2:4], xb.at[h, b, 1, 2:4], x_peer(1))

    def forward_lo(h, b):
        arrive(("lo", h, b))
        got["on_lo", h, b] = send(xb.at[h, b, 1, 0:2], xb.at[h, b, 2, 0:2], x_peer(1))

    def forward_hi(h, b):
        arrive(("hi", h, b))
        got["on_hi", h, b] = send(xb.at[h, b, 3, 2:4], xb.at[h, b, 2, 2:4], x_peer(3))

    def gate_up(h, b):
        arrive(*[(name, h, b) for name in ("lo", "hi", "lo2", "hi2", "on_lo", "on_hi")])

        def body(j, _):
            cols = pl.ds(pl.multiple_of(j * 256, 256), 256)
            rows = xb[h, b].reshape(128, COLS)
            gate = jnp.dot(rows, v_gate[:, cols], preferred_element_type=F32).astype(BF16)
            part[h, b, 0, 0, :, cols] = gate[:64]
            part[h, b, 1, 0, :, cols] = gate[64:]
            up = jnp.dot(rows, v_up[:, cols], preferred_element_type=F32).astype(BF16)
            part[h, b, 0, 1, :, cols] = up[:64]
            part[h, b, 1, 1, :, cols] = up[64:]
            return 0

        lax.fori_loop(0, 2, body, 0)
        got["core", h, b] = send(part.at[h, b, 1 - c], part_in.at[h, b], core_peer)

    def pair_sum(h, b):
        arrive(("core", h, b))
        pair[h, b] = (part[h, b, c].astype(F32) + part_in[h, b].astype(F32)).astype(BF16)
        got["pair", h, b] = send(pair.at[h, b], pair_in.at[h, b], pair_peer)

    def make_hidden(h, b):
        arrive(("pair", h, b))
        gate = pair[h, b, 0].astype(F32) + pair_in[h, b, 0].astype(F32)
        up = pair[h, b, 1].astype(F32) + pair_in[h, b, 1].astype(F32)
        hid[h, b, c] = (gate / (1.0 + jnp.exp(-gate)) * up).astype(BF16)
        got["hid", h, b] = send(hid.at[h, b, c], hid.at[h, b, c], core_peer)

    def heads_of(h, b):
        slots = slice(b * 4, b * 4 + 4)
        return (hf[:, slots] if h else hx[:, slots, yh]).reshape(128, 128)

    def project(h, b):
        arrive(("hid", h, b))
        arrive(*["head_y"] if h else [("head_x", d) for d in range(1, 4)])

        def body(j, _):
            cols = pl.ds(pl.multiple_of(j * 512, 512), 512)
            acc = jnp.dot(hid[h, b].reshape(128, HID), v_down[:, cols], preferred_element_type=F32)
            acc = acc + jnp.dot(heads_of(h, b), v_outw[:, cols], preferred_element_type=F32)
            po[h, b, :, :, :, cols] = acc.astype(BF16).reshape(NX, 4, ROWS, 512)
            return 0

        lax.fori_loop(0, 4, body, 0)
        got["r_lo", h, b] = send(po.at[h, b, 2, 0:2], relay.at[h, b, 0], x_peer(1))
        got["r_hi", h, b] = send(po.at[h, b, 2, 2:4], relay.at[h, b, 1], x_peer(3))
        got["d_hi", h, b] = send(po.at[h, b, 3, 2:4], direct.at[h, b, 0], x_peer(1))
        got["d_lo", h, b] = send(po.at[h, b, 1, 0:2], direct.at[h, b, 1], x_peer(3))

    def relay_lo(h, b):
        arrive(("r_lo", h, b))
        po[h, b, 3, 0:2] = (po[h, b, 3, 0:2].astype(F32) + relay[h, b, 0].astype(F32)).astype(BF16)
        got["m_lo", h, b] = send(po.at[h, b, 3, 0:2], merged.at[h, b, 0], x_peer(1))

    def relay_hi(h, b):
        arrive(("r_hi", h, b))
        po[h, b, 1, 2:4] = (po[h, b, 1, 2:4].astype(F32) + relay[h, b, 1].astype(F32)).astype(BF16)
        got["m_hi", h, b] = send(po.at[h, b, 1, 2:4], merged.at[h, b, 1], x_peer(3))

    def scatter_z(h, b, slots):
        for j in slots:
            d = (8 - SLOTS[b * 4 + j]) % 8
            if h == 1 and b == 0:
                peer = zy_peer(d) if d else y_peer
            elif d:
                peer = z_peer(d)
            else:
                continue
            got["s", h, b, j] = send(zs.at[h, b, j], zr.at[h, b, j], peer)

    def scatter_lo(h, b):
        arrive(("m_lo", h, b), ("d_lo", h, b))
        zs[h, b, 0:2] = (
            po[h, b, 0, 0:2].astype(F32) + merged[h, b, 0].astype(F32) + direct[h, b, 1].astype(F32)
        ).astype(BF16)
        scatter_z(h, b, (1, 0))

    def scatter_hi(h, b):
        arrive(("m_hi", h, b), ("d_hi", h, b))
        zs[h, b, 2:4] = (
            po[h, b, 0, 2:4].astype(F32) + merged[h, b, 1].astype(F32) + direct[h, b, 0].astype(F32)
        ).astype(BF16)
        scatter_z(h, b, (3, 2))

    def collect(acc, h, b, slots):
        for j in slots:
            arrive(("s", h, b, j))
            acc = acc + zr[h, b, j].astype(F32)
        return acc

    def finish_other():
        fin[...] = collect(jnp.zeros((ROWS, COLS), F32), 1, 1, range(4)).astype(BF16)
        got["last"] = send(fin, fin_in, y_peer)

    def sum_own():
        acc = zs[0, 0, 0].astype(F32)
        acc = collect(acc, 0, 1, range(4))
        acc = collect(acc, 0, 0, range(1, 4))
        return collect(acc, 1, 0, range(4))

    def send_heads():
        for d in range(1, 4):
            got["head_n", d] = send(hn.at[narrow], hn.at[narrow], n_peer(d))

    def turn_heads():
        arrive(*[("head_n", d) for d in range(1, 4)])
        for n in range(4):
            for b in range(2):
                rows = hn[n, b].astype(F32)
                ht[0, :, n * 2 + b, :] = rows[:, :128]
                ht[1, :, n * 2 + b, :] = rows[:, 128:]
        for half in range(2):
            hs[:, :, half] = ht[half].reshape(NZ, NX, 8, 128).astype(BF16)
        hz[:, 0] = hs[z]
        for s in range(1, 8):
            d = SLOTS[s]
            got["head_z", s] = send(hs.at[(z + d) % 8], hz.at[:, s], z_peer(d))

    def heads_x():
        arrive(*[("head_z", s) for s in range(1, 8)])
        hx[0] = hz[x]
        for d in (2, 1, 3):
            got["head_x", d] = send(hz.at[(x + d) % 4], hx.at[d], x_peer(d))

    def heads_y():
        arrive(*[("head_x", d) for d in range(1, 4)])
        got["head_y"] = send(hx.at[:, :, 1 - yh], hf, y_peer)

    swap()
    gather_z(1, 0)
    gather_z(0, 1)
    gather_z(1, 1)
    for load in loads[2:7]:
        load.wait()
    attend(0)
    gather_lo(1, 0)
    attend(1)
    send_heads()
    gather_hi(1, 0)
    gather_lo(0, 1)
    gather_z(0, 0)
    forward_lo(1, 0)
    gather_hi(0, 1)
    forward_hi(1, 0)
    turn_heads()
    gather_lo(1, 1)
    forward_lo(0, 1)
    forward_hi(0, 1)
    gather_hi(1, 1)
    for load in loads[7:]:
        load.wait()
    gate_up(1, 0)
    gather_lo(0, 0)
    pair_sum(1, 0)
    heads_x()
    gate_up(0, 1)
    forward_lo(1, 1)
    forward_hi(1, 1)
    gather_hi(0, 0)
    pair_sum(0, 1)
    make_hidden(1, 0)
    heads_y()
    forward_lo(0, 0)
    gate_up(1, 1)
    make_hidden(0, 1)
    forward_hi(0, 0)
    pair_sum(1, 1)
    project(0, 1)
    project(1, 0)
    gate_up(0, 0)
    make_hidden(1, 1)
    pair_sum(0, 0)
    relay_hi(0, 1)
    project(1, 1)
    relay_lo(1, 1)
    relay_lo(1, 0)
    scatter_hi(0, 1)
    relay_hi(1, 1)
    make_hidden(0, 0)
    relay_lo(0, 1)
    project(0, 0)
    relay_hi(1, 0)
    scatter_lo(1, 1)
    scatter_hi(1, 1)
    scatter_lo(0, 1)
    scatter_lo(1, 0)
    relay_hi(0, 0)
    relay_lo(0, 0)
    scatter_hi(1, 0)
    scatter_hi(0, 0)
    finish_other()
    scatter_lo(0, 0)
    own_half = sum_own()
    arrive("last")
    out[...] = (own_half + fin_in[...].astype(F32)).astype(BF16)

    for copy in started:
        copy.wait_send()


SENDS = 112


def local(*args):
    args = list(args)
    args[1] = args[1].reshape(1, COLS)
    anywhere = pl.BlockSpec(memory_space=pl.ANY)
    vm = pltpu.VMEM
    return pl.pallas_call(
        kernel,
        out_shape=jax.ShapeDtypeStruct((ROWS, COLS), BF16),
        in_specs=[anywhere] * 11 + [pl.BlockSpec(memory_space=pltpu.SMEM)],
        out_specs=pl.BlockSpec(memory_space=pltpu.VMEM),
        scratch_shapes=[
            vm((8, 8192), BF16),
            vm((1, COLS), F32),
            vm((2048, HID), BF16),
            vm((2048, HID), BF16),
            vm((HID, COLS), BF16),
            vm((128, COLS), BF16),
            vm((2, 8192), BF16),
            vm((2, HEAD_DIM), BF16),
            vm((2, HEAD_DIM), BF16),
            vm((2, 2048, HEAD_DIM), BF16),
            vm((2, 2048, HEAD_DIM), BF16),
            vm((2, HEADS, HEAD_DIM), F32),
            vm((2, 2, NX, 4, ROWS, COLS), BF16),
            vm((2, 2, 2, 2, 64, HID), BF16),
            vm((2, 2, 2, 64, HID), BF16),
            vm((2, 2, 2, 64, HID), BF16),
            vm((2, 2, 2, 64, HID), BF16),
            vm((2, 2, 2, 64, HID), BF16),
            vm((4, 2, HEADS, HEAD_DIM), BF16),
            vm((2, HEADS, 8, 128), F32),
            vm((NZ, NX, 2, 8, 128), BF16),
            vm((NX, NZ, 2, 8, 128), BF16),
            vm((NX, NZ, 2, 8, 128), BF16),
            vm((NX, NZ, 8, 128), BF16),
            vm((2, 2, NX, 4, ROWS, COLS), BF16),
            vm((2, 2, 2, 2, ROWS, COLS), BF16),
            vm((2, 2, 2, 2, ROWS, COLS), BF16),
            vm((2, 2, 2, 2, ROWS, COLS), BF16),
            vm((2, 2, 4, ROWS, COLS), BF16),
            vm((2, 2, 4, ROWS, COLS), BF16),
            vm((ROWS, COLS), BF16),
            vm((ROWS, COLS), BF16),
            pltpu.SemaphoreType.DMA((11,)),
            pltpu.SemaphoreType.DMA((SENDS,)),
            pltpu.SemaphoreType.DMA((SENDS,)),
        ],
        compiler_params=pltpu.CompilerParams(
            collective_id=0, has_side_effects=True, vmem_limit_bytes=56 * 1024 * 1024
        ),
    )(*args)


def solution(mesh):
    return jax.shard_map(
        local,
        mesh=mesh,
        in_specs=(
            P("wide", None),
            P("narrow"),
            P("narrow", "wide"),
            P("narrow", "wide"),
            P("wide", "narrow"),
            P("wide", "narrow"),
            P(("wide", "narrow"), None),
            P(("wide", "narrow"), None),
            P(("wide", "narrow"), None),
            P(("wide", "narrow"), None, None),
            P(("wide", "narrow"), None, None),
            P(("wide", "narrow")),
        ),
        out_specs=P("wide", "narrow"),
        check_vma=False,
    )
```

```python
import math

import jax
import jax.numpy as jnp
from jax import lax
from jax.experimental import pallas as pl
from jax.experimental.pallas import tpu as pltpu
from jax.sharding import PartitionSpec as P

HEADS = 32
HEAD_DIM = 256
NZ, NX = 8, 4
ROWS = 8
COLS = 2048
HID = 512
SLOTS = (0, 1, 7, 2, 6, 3, 5, 4)
FINAL = tuple((h, j) for h in range(2) for j in range(5) if h or j)

epsilon = 1e-05
masked_score = -1e30
F32 = jnp.float32
BF16 = jnp.bfloat16


def kernel(
    residual,
    norm_gain,
    gate_weight,
    up_weight,
    down_weight,
    out_weight,
    queries,
    key_fresh,
    value_fresh,
    key_cache,
    value_cache,
    lengths,
    out,
    v_res,
    v_gain,
    v_gate,
    v_up,
    v_down,
    v_outw,
    v_q,
    v_kf,
    v_vf,
    v_kc,
    v_vc,
    qh,
    xb,
    part,
    part_in,
    pair,
    pair_in,
    hid,
    hn,
    ht,
    hs,
    hz,
    hx,
    hf,
    po,
    relay,
    direct,
    merged,
    zs,
    zr,
    via_down,
    via_up,
    local_sem,
    send_sem,
    recv_sem,
):
    wide, narrow = lax.axis_index("wide"), lax.axis_index("narrow")
    z, x, yh = wide // 8, (wide // 2) % 4, wide % 2
    yl, c = narrow // 2, narrow % 2

    def at(z_, x_, yh_, n_):
        return ((z_ * 4 + x_) * 2 + yh_, n_)

    def z_peer(d):
        return at((z + d) % 8, x, yh, narrow)

    def x_peer(d):
        return at(z, (x + d) % 4, yh, narrow)

    y_peer = at(z, x, 1 - yh, narrow)

    def zy_peer(d):
        return at((z + d) % 8, x, 1 - yh, narrow)

    def n_peer(d):
        return at(z, x, yh, (narrow + d) % 4)

    core_peer = at(z, x, yh, yl * 2 + 1 - c)
    pair_peer = at(z, x, yh, (1 - yl) * 2 + c)

    names = [
        (residual, v_res),
        (norm_gain, v_gain),
        (queries, v_q),
        (key_fresh, v_kf),
        (value_fresh, v_vf),
        (key_cache, v_kc),
        (value_cache, v_vc),
        (gate_weight, v_gate),
        (up_weight, v_up),
        (out_weight, v_outw),
        (down_weight, v_down),
    ]
    loads = [
        pltpu.make_async_copy(src, dst, local_sem.at[i]) for i, (src, dst) in enumerate(names)
    ]
    (l_res, l_gain, l_q, l_kf, l_vf, l_kc, l_vc, l_gate, l_up, l_outw, l_down) = loads
    l_res.start()
    l_gain.start()

    peers = (
        [z_peer(d) for d in (4, 3, 5, 2, 6, 1, 7)]
        + [x_peer(d) for d in range(1, 4)]
        + [y_peer]
        + [zy_peer(d) for d in (1, 7, 2, 6)]
        + [n_peer(d) for d in range(1, 4)]
    )
    barrier = pltpu.get_barrier_semaphore()
    for peer in peers:
        pl.semaphore_signal(barrier, inc=1, device_id=peer, device_id_type=pl.DeviceIdType.MESH)

    started = []

    def send(src, dst, peer):
        k = len(started)
        copy = pltpu.make_async_remote_copy(
            src_ref=src,
            dst_ref=dst,
            send_sem=send_sem.at[k],
            recv_sem=recv_sem.at[k],
            device_id=peer,
            device_id_type=pl.DeviceIdType.MESH,
        )
        copy.start()
        started.append(copy)
        return copy

    got = {}
    waited = set()

    def arrive(*keys):
        for key in keys:
            if key in got and key not in waited:
                got[key].wait_recv()
                waited.add(key)

    l_res.wait()
    l_gain.wait()
    for load in loads[2:]:
        load.start()
    stream = v_res[...].astype(F32)
    row_mean = jnp.mean(stream, axis=1, keepdims=True)
    centered = stream - row_mean
    row_var = jnp.mean(centered * centered, axis=1, keepdims=True)
    own = v_res[:, pl.ds(pl.multiple_of(narrow * COLS, COLS), COLS)].astype(F32) - row_mean
    normed = own * lax.rsqrt(row_var + epsilon) * v_gain[...]
    xb[0, 0, 0, 0] = normed.astype(BF16)

    pl.semaphore_wait(barrier, len(peers))

    def swap():
        got["swap"] = send(xb.at[0, 0, 0, 0], xb.at[1, 0, 0, 0], y_peer)

    def gather_z(h, b):
        if h == 1 and b == 1:
            arrive("swap")
        straight = h == 1 and b == 0
        for j in range(4):
            d = SLOTS[b * 4 + j]
            if d:
                got["z", h, b, j] = send(
                    xb.at[0 if straight else h, 0, 0, 0],
                    xb.at[h, b, 0, j],
                    zy_peer(d) if straight else z_peer(d),
                )

    scale = 1.0 / math.sqrt(HEAD_DIM)

    def attend(b):
        for head in range(HEADS):
            qh[b, head : head + 1, :] = v_q[b : b + 1, head * HEAD_DIM : (head + 1) * HEAD_DIM].astype(F32)
        query = qh[b]
        scores = (
            lax.dot_general(
                query.astype(BF16), v_kc[b], (((1,), (1,)), ((), ())), preferred_element_type=F32
            )
            * scale
        )
        fresh = jnp.sum(query * v_kf[b : b + 1, :].astype(F32), axis=1, keepdims=True) * scale
        position = lax.broadcasted_iota(jnp.int32, scores.shape, 1)
        masked = jnp.where(position < lengths[b], scores, masked_score)
        peak = jnp.maximum(jnp.max(masked, axis=1, keepdims=True), fresh)
        weights = jnp.exp(masked - peak).astype(BF16)
        fresh_weight = jnp.exp(fresh - peak).astype(BF16).astype(F32)
        total = jnp.sum(weights.astype(F32), axis=1, keepdims=True) + fresh_weight
        mixed = jnp.dot(weights, v_vc[b], preferred_element_type=F32)
        mixed = mixed + fresh_weight * v_vf[b : b + 1, :].astype(F32)
        hn[narrow, b] = (mixed / total).astype(BF16)

    def gather_lo(h, b):
        if h == 1 and b == 0:
            arrive("swap")
        arrive(("z", h, b, 0), ("z", h, b, 1))
        got["lo", h, b] = send(xb.at[h, b, 0, 0:2], xb.at[h, b, 1, 0:2], x_peer(1))
        got["hi2", h, b] = send(xb.at[h, b, 0, 0:2], xb.at[h, b, 3, 0:2], x_peer(3))

    def gather_hi(h, b):
        arrive(("z", h, b, 2), ("z", h, b, 3))
        got["hi", h, b] = send(xb.at[h, b, 0, 2:4], xb.at[h, b, 3, 2:4], x_peer(3))
        got["lo2", h, b] = send(xb.at[h, b, 0, 2:4], xb.at[h, b, 1, 2:4], x_peer(1))

    def forward_lo(h, b):
        arrive(("lo", h, b))
        got["on_lo", h, b] = send(xb.at[h, b, 1, 0:2], xb.at[h, b, 2, 0:2], x_peer(1))

    def forward_hi(h, b):
        arrive(("hi", h, b))
        got["on_hi", h, b] = send(xb.at[h, b, 3, 2:4], xb.at[h, b, 2, 2:4], x_peer(3))

    def gate_up(h, b):
        arrive(*[(name, h, b) for name in ("lo", "hi", "lo2", "hi2", "on_lo", "on_hi")])

        def body(j, _):
            cols = pl.ds(pl.multiple_of(j * 256, 256), 256)
            rows = xb[h, b].reshape(128, COLS)
            gate = jnp.dot(rows, v_gate[:, cols], preferred_element_type=F32).astype(BF16)
            part[h, b, 0, 0, :, cols] = gate[:64]
            part[h, b, 1, 0, :, cols] = gate[64:]
            up = jnp.dot(rows, v_up[:, cols], preferred_element_type=F32).astype(BF16)
            part[h, b, 0, 1, :, cols] = up[:64]
            part[h, b, 1, 1, :, cols] = up[64:]
            return 0

        lax.fori_loop(0, 2, body, 0)
        got["core", h, b] = send(part.at[h, b, 1 - c], part_in.at[h, b], core_peer)

    def pair_sum(h, b):
        arrive(("core", h, b))
        pair[h, b] = (part[h, b, c].astype(F32) + part_in[h, b].astype(F32)).astype(BF16)
        got["pair", h, b] = send(pair.at[h, b], pair_in.at[h, b], pair_peer)

    def make_hidden(h, b):
        arrive(("pair", h, b))
        gate = pair[h, b, 0].astype(F32) + pair_in[h, b, 0].astype(F32)
        up = pair[h, b, 1].astype(F32) + pair_in[h, b, 1].astype(F32)
        hid[h, b, c] = (gate / (1.0 + jnp.exp(-gate)) * up).astype(BF16)
        got["hid", h, b] = send(hid.at[h, b, c], hid.at[h, b, c], core_peer)

    def heads_of(h, b):
        slots = slice(b * 4, b * 4 + 4)
        return (hf[:, slots] if h else hx[:, slots, yh]).reshape(128, 128)

    def project(h, b):
        arrive(("hid", h, b))
        arrive(*["head_y"] if h else [("head_x", d) for d in range(1, 4)])

        def body(j, _):
            cols = pl.ds(pl.multiple_of(j * 512, 512), 512)
            acc = jnp.dot(hid[h, b].reshape(128, HID), v_down[:, cols], preferred_element_type=F32)
            acc = acc + jnp.dot(heads_of(h, b), v_outw[:, cols], preferred_element_type=F32)
            po[h, b, :, :, :, cols] = acc.astype(BF16).reshape(NX, 4, ROWS, 512)
            return 0

        lax.fori_loop(0, 4, body, 0)
        got["r_lo", h, b] = send(po.at[h, b, 2, 0:2], relay.at[h, b, 0], x_peer(1))
        got["r_hi", h, b] = send(po.at[h, b, 2, 2:4], relay.at[h, b, 1], x_peer(3))
        got["d_hi", h, b] = send(po.at[h, b, 3, 2:4], direct.at[h, b, 0], x_peer(1))
        got["d_lo", h, b] = send(po.at[h, b, 1, 0:2], direct.at[h, b, 1], x_peer(3))

    def relay_lo(h, b):
        arrive(("r_lo", h, b))
        po[h, b, 3, 0:2] = (po[h, b, 3, 0:2].astype(F32) + relay[h, b, 0].astype(F32)).astype(BF16)
        got["m_lo", h, b] = send(po.at[h, b, 3, 0:2], merged.at[h, b, 0], x_peer(1))

    def relay_hi(h, b):
        arrive(("r_hi", h, b))
        po[h, b, 1, 2:4] = (po[h, b, 1, 2:4].astype(F32) + relay[h, b, 1].astype(F32)).astype(BF16)
        got["m_hi", h, b] = send(po.at[h, b, 1, 2:4], merged.at[h, b, 1], x_peer(3))

    def z_home(h, d):
        if h == 0:
            return z_peer(d)
        return zy_peer(d) if d else y_peer

    def sums_lo(h, b):
        arrive(("m_lo", h, b), ("d_lo", h, b))
        zs[h, b, 0:2] = (
            po[h, b, 0, 0:2].astype(F32) + merged[h, b, 0].astype(F32) + direct[h, b, 1].astype(F32)
        ).astype(BF16)

    def sums_hi(h, b):
        arrive(("m_hi", h, b), ("d_hi", h, b))
        zs[h, b, 2:4] = (
            po[h, b, 0, 2:4].astype(F32) + merged[h, b, 1].astype(F32) + direct[h, b, 0].astype(F32)
        ).astype(BF16)

    def scatter_lo(h, b):
        sums_lo(h, b)
        if b == 0:
            got["s", h, 1] = send(zs.at[h, 0, 1], zr.at[h, 1], z_home(h, 7))
            if h == 1:
                got["s", h, 0] = send(zs.at[h, 0, 0], zr.at[h, 0], y_peer)
        else:
            got["via", h, 3] = send(zs.at[h, 1, 1], via_down.at[h, 0], z_peer(7))

    def scatter_hi(h, b):
        sums_hi(h, b)
        half = COLS // 2
        if b == 0:
            got["s", h, 2] = send(zs.at[h, 0, 2], zr.at[h, 2], z_home(h, 1))
        else:
            got["via", h, 5] = send(zs.at[h, 1, 2], via_up.at[h, 0], z_peer(1))
            got["via", h, "4a"] = send(
                zs.at[h, 1, 3, :, 0:half], via_down.at[h, 1, :, 0:half], z_peer(6)
            )
            got["via", h, "4b"] = send(
                zs.at[h, 1, 3, :, half:COLS], via_up.at[h, 1, :, half:COLS], z_peer(2)
            )

    def scatter_down(h, b):
        arrive(("via", h, 3), ("via", h, "4a"))
        half = COLS // 2
        acc = zs[h, 0, 3].astype(F32) + via_down[h, 0].astype(F32)
        zs[h, 0, 3, :, half:COLS] = acc[:, half:COLS].astype(BF16)
        zs[h, 0, 3, :, 0:half] = (
            acc[:, 0:half] + via_down[h, 1, :, 0:half].astype(F32)
        ).astype(BF16)
        got["s", h, 3] = send(zs.at[h, 0, 3], zr.at[h, 3], z_home(h, 6))

    def scatter_up(h, b):
        arrive(("via", h, 5), ("via", h, "4b"))
        half = COLS // 2
        acc = zs[h, 1, 0].astype(F32) + via_up[h, 0].astype(F32)
        zs[h, 1, 0, :, 0:half] = acc[:, 0:half].astype(BF16)
        zs[h, 1, 0, :, half:COLS] = (
            acc[:, half:COLS] + via_up[h, 1, :, half:COLS].astype(F32)
        ).astype(BF16)
        got["s", h, 4] = send(zs.at[h, 1, 0], zr.at[h, 4], z_home(h, 2))

    def sum_own():
        acc = zs[0, 0, 0].astype(F32)
        for h, j in FINAL:
            arrive(("s", h, j))
            acc = acc + zr[h, j].astype(F32)
        return acc

    def send_heads():
        for d in range(1, 4):
            got["head_n", d] = send(hn.at[narrow], hn.at[narrow], n_peer(d))

    def turn_heads():
        arrive(*[("head_n", d) for d in range(1, 4)])
        for n in range(4):
            for b in range(2):
                rows = hn[n, b].astype(F32)
                ht[0, :, n * 2 + b, :] = rows[:, :128]
                ht[1, :, n * 2 + b, :] = rows[:, 128:]
        for half in range(2):
            hs[:, :, half] = ht[half].reshape(NZ, NX, 8, 128).astype(BF16)
        hz[:, 0] = hs[z]
        for s in range(1, 8):
            d = SLOTS[s]
            got["head_z", s] = send(hs.at[(z + d) % 8], hz.at[:, s], z_peer(d))

    def heads_x():
        arrive(*[("head_z", s) for s in range(1, 8)])
        hx[0] = hz[x]
        for d in (2, 1, 3):
            got["head_x", d] = send(hz.at[(x + d) % 4], hx.at[d], x_peer(d))

    def heads_y():
        arrive(*[("head_x", d) for d in range(1, 4)])
        got["head_y"] = send(hx.at[:, :, 1 - yh], hf, y_peer)

    swap()
    gather_z(1, 0)
    gather_z(0, 1)
    for load in loads[2:7]:
        load.wait()
    attend(0)
    attend(1)
    send_heads()
    gather_z(1, 1)
    turn_heads()
    gather_lo(1, 0)
    gather_hi(1, 0)
    gather_lo(0, 1)
    forward_lo(1, 0)
    gather_hi(0, 1)
    forward_hi(1, 0)
    gather_z(0, 0)
    forward_lo(0, 1)
    gather_lo(1, 1)
    forward_hi(0, 1)
    gather_hi(1, 1)
    gather_lo(0, 0)
    for load in loads[7:]:
        load.wait()
    gate_up(1, 0)
    pair_sum(1, 0)
    heads_x()
    forward_lo(1, 1)
    gate_up(0, 1)
    forward_hi(1, 1)
    gather_hi(0, 0)
    pair_sum(0, 1)
    heads_y()
    forward_lo(0, 0)
    gate_up(1, 1)
    make_hidden(1, 0)
    forward_hi(0, 0)
    make_hidden(0, 1)
    pair_sum(1, 1)
    project(0, 1)
    project(1, 0)
    gate_up(0, 0)
    make_hidden(1, 1)
    pair_sum(0, 0)
    project(1, 1)
    relay_hi(0, 1)
    relay_lo(1, 0)
    relay_lo(0, 1)
    make_hidden(0, 0)
    relay_hi(1, 1)
    relay_lo(1, 1)
    project(0, 0)
    scatter_hi(0, 1)
    relay_hi(1, 0)
    scatter_lo(1, 0)
    scatter_hi(1, 1)
    scatter_lo(1, 1)
    scatter_lo(0, 1)
    relay_hi(0, 0)
    relay_lo(0, 0)
    scatter_hi(1, 0)
    scatter_up(1, 1)
    scatter_down(1, 0)
    scatter_up(0, 1)
    scatter_hi(0, 0)
    scatter_down(0, 0)
    scatter_lo(0, 0)
    out[...] = sum_own().astype(BF16)

    for copy in started:
        copy.wait_send()


SENDS = 112


def local(*args):
    args = list(args)
    args[1] = args[1].reshape(1, COLS)
    anywhere = pl.BlockSpec(memory_space=pl.ANY)
    vm = pltpu.VMEM
    return pl.pallas_call(
        kernel,
        out_shape=jax.ShapeDtypeStruct((ROWS, COLS), BF16),
        in_specs=[anywhere] * 11 + [pl.BlockSpec(memory_space=pltpu.SMEM)],
        out_specs=pl.BlockSpec(memory_space=pltpu.VMEM),
        scratch_shapes=[
            vm((8, 8192), BF16),
            vm((1, COLS), F32),
            vm((2048, HID), BF16),
            vm((2048, HID), BF16),
            vm((HID, COLS), BF16),
            vm((128, COLS), BF16),
            vm((2, 8192), BF16),
            vm((2, HEAD_DIM), BF16),
            vm((2, HEAD_DIM), BF16),
            vm((2, 2048, HEAD_DIM), BF16),
            vm((2, 2048, HEAD_DIM), BF16),
            vm((2, HEADS, HEAD_DIM), F32),
            vm((2, 2, NX, 4, ROWS, COLS), BF16),
            vm((2, 2, 2, 2, 64, HID), BF16),
            vm((2, 2, 2, 64, HID), BF16),
            vm((2, 2, 2, 64, HID), BF16),
            vm((2, 2, 2, 64, HID), BF16),
            vm((2, 2, 2, 64, HID), BF16),
            vm((4, 2, HEADS, HEAD_DIM), BF16),
            vm((2, HEADS, 8, 128), F32),
            vm((NZ, NX, 2, 8, 128), BF16),
            vm((NX, NZ, 2, 8, 128), BF16),
            vm((NX, NZ, 2, 8, 128), BF16),
            vm((NX, NZ, 8, 128), BF16),
            vm((2, 2, NX, 4, ROWS, COLS), BF16),
            vm((2, 2, 2, 2, ROWS, COLS), BF16),
            vm((2, 2, 2, 2, ROWS, COLS), BF16),
            vm((2, 2, 2, 2, ROWS, COLS), BF16),
            vm((2, 2, 4, ROWS, COLS), BF16),
            vm((2, 5, ROWS, COLS), BF16),
            vm((2, 2, ROWS, COLS), BF16),
            vm((2, 2, ROWS, COLS), BF16),
            pltpu.SemaphoreType.DMA((11,)),
            pltpu.SemaphoreType.DMA((SENDS,)),
            pltpu.SemaphoreType.DMA((SENDS,)),
        ],
        compiler_params=pltpu.CompilerParams(
            collective_id=0, has_side_effects=True, vmem_limit_bytes=56 * 1024 * 1024
        ),
    )(*args)


def solution(mesh):
    return jax.shard_map(
        local,
        mesh=mesh,
        in_specs=(
            P("wide", None),
            P("narrow"),
            P("narrow", "wide"),
            P("narrow", "wide"),
            P("wide", "narrow"),
            P("wide", "narrow"),
            P(("wide", "narrow"), None),
            P(("wide", "narrow"), None),
            P(("wide", "narrow"), None),
            P(("wide", "narrow"), None, None),
            P(("wide", "narrow"), None, None),
            P(("wide", "narrow")),
        ),
        out_specs=P("wide", "narrow"),
        check_vma=False,
    )
```

```python
import math

import jax
import jax.numpy as jnp
from jax import lax
from jax.experimental import pallas as pl
from jax.experimental.pallas import tpu as pltpu
from jax.sharding import PartitionSpec as P

HEADS = 32
HEAD_DIM = 256
NZ, NX = 8, 4
ROWS = 8
COLS = 2048
HID = 512
SLOTS = (0, 1, 7, 2, 6, 3, 5, 4)
FINAL = tuple((h, j) for h in range(2) for j in range(5) if h or j)

epsilon = 1e-05
masked_score = -1e30
F32 = jnp.float32
BF16 = jnp.bfloat16


def kernel(
    residual,
    norm_gain,
    gate_weight,
    up_weight,
    down_weight,
    out_weight,
    queries,
    key_fresh,
    value_fresh,
    key_cache,
    value_cache,
    lengths,
    out,
    v_res,
    v_gain,
    v_gate,
    v_up,
    v_down,
    v_outw,
    v_q,
    v_kf,
    v_vf,
    v_kc,
    v_vc,
    qh,
    xb,
    part,
    part_in,
    pair,
    pair_in,
    hid,
    hn,
    ht,
    hs,
    hz,
    hx,
    hf,
    po,
    relay,
    direct,
    merged,
    zs,
    zr,
    via_down,
    via_up,
    local_sem,
    send_sem,
    recv_sem,
):
    wide, narrow = lax.axis_index("wide"), lax.axis_index("narrow")
    z, x, yh = wide // 8, (wide // 2) % 4, wide % 2
    yl, c = narrow // 2, narrow % 2

    def at(z_, x_, yh_, n_):
        return ((z_ * 4 + x_) * 2 + yh_, n_)

    def z_peer(d):
        return at((z + d) % 8, x, yh, narrow)

    def x_peer(d):
        return at(z, (x + d) % 4, yh, narrow)

    y_peer = at(z, x, 1 - yh, narrow)

    def zy_peer(d):
        return at((z + d) % 8, x, 1 - yh, narrow)

    def n_peer(d):
        return at(z, x, yh, (narrow + d) % 4)

    core_peer = at(z, x, yh, yl * 2 + 1 - c)
    pair_peer = at(z, x, yh, (1 - yl) * 2 + c)

    names = [
        (residual, v_res),
        (norm_gain, v_gain),
        (queries, v_q),
        (key_fresh, v_kf),
        (value_fresh, v_vf),
        (key_cache, v_kc),
        (value_cache, v_vc),
        (gate_weight, v_gate),
        (up_weight, v_up),
        (out_weight, v_outw),
        (down_weight, v_down),
    ]
    loads = [
        pltpu.make_async_copy(src, dst, local_sem.at[i]) for i, (src, dst) in enumerate(names)
    ]
    (l_res, l_gain, l_q, l_kf, l_vf, l_kc, l_vc, l_gate, l_up, l_outw, l_down) = loads
    l_res.start()
    l_gain.start()

    peers = (
        [z_peer(d) for d in (4, 3, 5, 2, 6, 1, 7)]
        + [x_peer(d) for d in range(1, 4)]
        + [y_peer]
        + [zy_peer(d) for d in (1, 7, 2, 6)]
        + [n_peer(d) for d in range(1, 4)]
    )
    barrier = pltpu.get_barrier_semaphore()
    for peer in peers:
        pl.semaphore_signal(barrier, inc=1, device_id=peer, device_id_type=pl.DeviceIdType.MESH)

    started = []

    def send(src, dst, peer):
        k = len(started)
        copy = pltpu.make_async_remote_copy(
            src_ref=src,
            dst_ref=dst,
            send_sem=send_sem.at[k],
            recv_sem=recv_sem.at[k],
            device_id=peer,
            device_id_type=pl.DeviceIdType.MESH,
        )
        copy.start()
        started.append(copy)
        return copy

    got = {}
    waited = set()

    def arrive(*keys):
        for key in keys:
            if key in got and key not in waited:
                got[key].wait_recv()
                waited.add(key)

    l_res.wait()
    l_gain.wait()
    for load in loads[2:]:
        load.start()
    stream = v_res[...].astype(F32)
    row_mean = jnp.mean(stream, axis=1, keepdims=True)
    centered = stream - row_mean
    row_var = jnp.mean(centered * centered, axis=1, keepdims=True)
    own = v_res[:, pl.ds(pl.multiple_of(narrow * COLS, COLS), COLS)].astype(F32) - row_mean
    normed = own * lax.rsqrt(row_var + epsilon) * v_gain[...]
    xb[0, 0, 0, 0] = normed.astype(BF16)

    pl.semaphore_wait(barrier, len(peers))

    def swap():
        got["swap"] = send(xb.at[0, 0, 0, 0], xb.at[1, 0, 0, 0], y_peer)

    def gather_z(h, b):
        for slot in range(1, 5):
            d = SLOTS[slot]
            got["z", h, slot // 4, slot % 4] = send(
                xb.at[0, 0, 0, 0],
                xb.at[h, slot // 4, 0, slot % 4],
                zy_peer(d) if h else z_peer(d),
            )

    half = COLS // 2

    def gather_up(h, b):
        arrive(("z", h, 0, 3))
        got["z", h, 1, 1] = send(xb.at[h, 0, 0, 3], xb.at[h, 1, 0, 1], z_peer(1))
        got["z", h, 1, 3] = send(
            xb.at[h, 0, 0, 3, :, 0:half], xb.at[h, 1, 0, 3, :, 0:half], z_peer(2)
        )

    def gather_down(h, b):
        arrive(("z", h, 1, 0))
        got["z", h, 1, 2] = send(xb.at[h, 1, 0, 0], xb.at[h, 1, 0, 2], z_peer(7))
        got["z", h, 1, 4] = send(
            xb.at[h, 1, 0, 0, :, half:COLS], xb.at[h, 1, 0, 3, :, half:COLS], z_peer(6)
        )

    scale = 1.0 / math.sqrt(HEAD_DIM)

    def attend(b):
        for head in range(HEADS):
            qh[b, head : head + 1, :] = v_q[b : b + 1, head * HEAD_DIM : (head + 1) * HEAD_DIM].astype(F32)
        query = qh[b]
        scores = (
            lax.dot_general(
                query.astype(BF16), v_kc[b], (((1,), (1,)), ((), ())), preferred_element_type=F32
            )
            * scale
        )
        fresh = jnp.sum(query * v_kf[b : b + 1, :].astype(F32), axis=1, keepdims=True) * scale
        position = lax.broadcasted_iota(jnp.int32, scores.shape, 1)
        masked = jnp.where(position < lengths[b], scores, masked_score)
        peak = jnp.maximum(jnp.max(masked, axis=1, keepdims=True), fresh)
        weights = jnp.exp(masked - peak).astype(BF16)
        fresh_weight = jnp.exp(fresh - peak).astype(BF16).astype(F32)
        total = jnp.sum(weights.astype(F32), axis=1, keepdims=True) + fresh_weight
        mixed = jnp.dot(weights, v_vc[b], preferred_element_type=F32)
        mixed = mixed + fresh_weight * v_vf[b : b + 1, :].astype(F32)
        hn[narrow, b] = (mixed / total).astype(BF16)

    def gather_lo(h, b):
        if h == 1 and b == 0:
            arrive("swap")
        arrive(("z", h, b, 0), ("z", h, b, 1))
        got["lo", h, b] = send(xb.at[h, b, 0, 0:2], xb.at[h, b, 1, 0:2], x_peer(1))
        got["hi2", h, b] = send(xb.at[h, b, 0, 0:2], xb.at[h, b, 3, 0:2], x_peer(3))

    def gather_hi(h, b):
        arrive(("z", h, b, 2), ("z", h, b, 3), ("z", h, b, 4))
        got["hi", h, b] = send(xb.at[h, b, 0, 2:4], xb.at[h, b, 3, 2:4], x_peer(3))
        got["lo2", h, b] = send(xb.at[h, b, 0, 2:4], xb.at[h, b, 1, 2:4], x_peer(1))

    def forward_lo(h, b):
        arrive(("lo", h, b))
        got["on_lo", h, b] = send(xb.at[h, b, 1, 0:2], xb.at[h, b, 2, 0:2], x_peer(1))

    def forward_hi(h, b):
        arrive(("hi", h, b))
        got["on_hi", h, b] = send(xb.at[h, b, 3, 2:4], xb.at[h, b, 2, 2:4], x_peer(3))

    def gate_up(h, b):
        arrive(*[(name, h, b) for name in ("lo", "hi", "lo2", "hi2", "on_lo", "on_hi")])

        def body(j, _):
            cols = pl.ds(pl.multiple_of(j * 256, 256), 256)
            rows = xb[h, b].reshape(128, COLS)
            gate = jnp.dot(rows, v_gate[:, cols], preferred_element_type=F32).astype(BF16)
            part[h, b, 0, 0, :, cols] = gate[:64]
            part[h, b, 1, 0, :, cols] = gate[64:]
            up = jnp.dot(rows, v_up[:, cols], preferred_element_type=F32).astype(BF16)
            part[h, b, 0, 1, :, cols] = up[:64]
            part[h, b, 1, 1, :, cols] = up[64:]
            return 0

        lax.fori_loop(0, 2, body, 0)
        got["core", h, b] = send(part.at[h, b, 1 - c], part_in.at[h, b], core_peer)

    def pair_sum(h, b):
        arrive(("core", h, b))
        pair[h, b] = (part[h, b, c].astype(F32) + part_in[h, b].astype(F32)).astype(BF16)
        got["pair", h, b] = send(pair.at[h, b], pair_in.at[h, b], pair_peer)

    def make_hidden(h, b):
        arrive(("pair", h, b))
        gate = pair[h, b, 0].astype(F32) + pair_in[h, b, 0].astype(F32)
        up = pair[h, b, 1].astype(F32) + pair_in[h, b, 1].astype(F32)
        hid[h, b, c] = (gate / (1.0 + jnp.exp(-gate)) * up).astype(BF16)
        got["hid", h, b] = send(hid.at[h, b, c], hid.at[h, b, c], core_peer)

    def heads_of(h, b):
        slots = slice(b * 4, b * 4 + 4)
        return (hf[:, slots] if h else hx[:, slots, yh]).reshape(128, 128)

    def project(h, b):
        arrive(("hid", h, b))
        arrive(*["head_y"] if h else [("head_x", d) for d in range(1, 4)])

        def body(j, _):
            cols = pl.ds(pl.multiple_of(j * 512, 512), 512)
            acc = jnp.dot(hid[h, b].reshape(128, HID), v_down[:, cols], preferred_element_type=F32)
            acc = acc + jnp.dot(heads_of(h, b), v_outw[:, cols], preferred_element_type=F32)
            po[h, b, :, :, :, cols] = acc.astype(BF16).reshape(NX, 4, ROWS, 512)
            return 0

        lax.fori_loop(0, 4, body, 0)
        got["r_lo", h, b] = send(po.at[h, b, 2, 0:2], relay.at[h, b, 0], x_peer(1))
        got["r_hi", h, b] = send(po.at[h, b, 2, 2:4], relay.at[h, b, 1], x_peer(3))
        got["d_hi", h, b] = send(po.at[h, b, 3, 2:4], direct.at[h, b, 0], x_peer(1))
        got["d_lo", h, b] = send(po.at[h, b, 1, 0:2], direct.at[h, b, 1], x_peer(3))

    def relay_lo(h, b):
        arrive(("r_lo", h, b))
        po[h, b, 3, 0:2] = (po[h, b, 3, 0:2].astype(F32) + relay[h, b, 0].astype(F32)).astype(BF16)
        got["m_lo", h, b] = send(po.at[h, b, 3, 0:2], merged.at[h, b, 0], x_peer(1))

    def relay_hi(h, b):
        arrive(("r_hi", h, b))
        po[h, b, 1, 2:4] = (po[h, b, 1, 2:4].astype(F32) + relay[h, b, 1].astype(F32)).astype(BF16)
        got["m_hi", h, b] = send(po.at[h, b, 1, 2:4], merged.at[h, b, 1], x_peer(3))

    def z_home(h, d):
        if h == 0:
            return z_peer(d)
        return zy_peer(d) if d else y_peer

    def sums_lo(h, b):
        arrive(("m_lo", h, b), ("d_lo", h, b))
        zs[h, b, 0:2] = (
            po[h, b, 0, 0:2].astype(F32) + merged[h, b, 0].astype(F32) + direct[h, b, 1].astype(F32)
        ).astype(BF16)

    def sums_hi(h, b):
        arrive(("m_hi", h, b), ("d_hi", h, b))
        zs[h, b, 2:4] = (
            po[h, b, 0, 2:4].astype(F32) + merged[h, b, 1].astype(F32) + direct[h, b, 0].astype(F32)
        ).astype(BF16)

    def scatter_lo(h, b):
        sums_lo(h, b)
        if b == 0:
            got["s", h, 1] = send(zs.at[h, 0, 1], zr.at[h, 1], z_home(h, 7))
            if h == 1:
                got["s", h, 0] = send(zs.at[h, 0, 0], zr.at[h, 0], y_peer)
        else:
            got["via", h, 3] = send(zs.at[h, 1, 1], via_down.at[h, 0], z_peer(7))

    def scatter_hi(h, b):
        sums_hi(h, b)
        half = COLS // 2
        if b == 0:
            got["s", h, 2] = send(zs.at[h, 0, 2], zr.at[h, 2], z_home(h, 1))
        else:
            got["via", h, 5] = send(zs.at[h, 1, 2], via_up.at[h, 0], z_peer(1))
            got["via", h, "4a"] = send(
                zs.at[h, 1, 3, :, 0:half], via_down.at[h, 1, :, 0:half], z_peer(6)
            )
            got["via", h, "4b"] = send(
                zs.at[h, 1, 3, :, half:COLS], via_up.at[h, 1, :, half:COLS], z_peer(2)
            )

    def scatter_down(h, b):
        arrive(("via", h, 3), ("via", h, "4a"))
        half = COLS // 2
        acc = zs[h, 0, 3].astype(F32) + via_down[h, 0].astype(F32)
        zs[h, 0, 3, :, half:COLS] = acc[:, half:COLS].astype(BF16)
        zs[h, 0, 3, :, 0:half] = (
            acc[:, 0:half] + via_down[h, 1, :, 0:half].astype(F32)
        ).astype(BF16)
        got["s", h, 3] = send(zs.at[h, 0, 3], zr.at[h, 3], z_home(h, 6))

    def scatter_up(h, b):
        arrive(("via", h, 5), ("via", h, "4b"))
        half = COLS // 2
        acc = zs[h, 1, 0].astype(F32) + via_up[h, 0].astype(F32)
        zs[h, 1, 0, :, 0:half] = acc[:, 0:half].astype(BF16)
        zs[h, 1, 0, :, half:COLS] = (
            acc[:, half:COLS] + via_up[h, 1, :, half:COLS].astype(F32)
        ).astype(BF16)
        got["s", h, 4] = send(zs.at[h, 1, 0], zr.at[h, 4], z_home(h, 2))

    def sum_own():
        acc = zs[0, 0, 0].astype(F32)
        for h, j in FINAL:
            arrive(("s", h, j))
            acc = acc + zr[h, j].astype(F32)
        return acc

    def send_heads():
        for d in range(1, 4):
            got["head_n", d] = send(hn.at[narrow], hn.at[narrow], n_peer(d))

    def turn_heads():
        arrive(*[("head_n", d) for d in range(1, 4)])
        for n in range(4):
            for b in range(2):
                rows = hn[n, b].astype(F32)
                ht[0, :, n * 2 + b, :] = rows[:, :128]
                ht[1, :, n * 2 + b, :] = rows[:, 128:]
        for half in range(2):
            hs[:, :, half] = ht[half].reshape(NZ, NX, 8, 128).astype(BF16)
        hz[:, 0] = hs[z]
        for s in range(1, 8):
            d = SLOTS[s]
            got["head_z", s] = send(hs.at[(z + d) % 8], hz.at[:, s], z_peer(d))

    def heads_x():
        arrive(*[("head_z", s) for s in range(1, 8)])
        hx[0] = hz[x]
        for d in (2, 1, 3):
            got["head_x", d] = send(hz.at[(x + d) % 4], hx.at[d], x_peer(d))

    def heads_y():
        arrive(*[("head_x", d) for d in range(1, 4)])
        got["head_y"] = send(hx.at[:, :, 1 - yh], hf, y_peer)

    swap()
    gather_z(1, 0)
    gather_z(0, 0)
    for load in loads[2:7]:
        load.wait()
    attend(0)
    gather_lo(1, 0)
    attend(1)
    send_heads()
    gather_up(1, 1)
    gather_hi(1, 0)
    gather_up(0, 1)
    gather_hi(0, 0)
    gather_down(1, 1)
    forward_lo(1, 0)
    gather_lo(1, 1)
    gather_down(0, 1)
    forward_hi(1, 0)
    turn_heads()
    gather_hi(1, 1)
    gather_lo(0, 1)
    gather_hi(0, 1)
    forward_lo(1, 1)
    forward_hi(1, 1)
    heads_x()
    for load in loads[7:]:
        load.wait()
    gate_up(1, 0)
    pair_sum(1, 0)
    forward_lo(0, 1)
    forward_hi(0, 1)
    forward_hi(0, 0)
    gather_lo(0, 0)
    gate_up(1, 1)
    heads_y()
    pair_sum(1, 1)
    gate_up(0, 1)
    forward_lo(0, 0)
    make_hidden(1, 0)
    pair_sum(0, 1)
    project(1, 0)
    make_hidden(1, 1)
    gate_up(0, 0)
    project(1, 1)
    make_hidden(0, 1)
    pair_sum(0, 0)
    project(0, 1)
    relay_lo(1, 1)
    relay_lo(1, 0)
    relay_hi(1, 1)
    make_hidden(0, 0)
    relay_hi(0, 1)
    relay_lo(0, 1)
    project(0, 0)
    relay_hi(1, 0)
    scatter_hi(1, 1)
    scatter_lo(1, 1)
    scatter_lo(1, 0)
    scatter_hi(0, 1)
    relay_hi(0, 0)
    scatter_lo(0, 1)
    relay_lo(0, 0)
    scatter_up(1, 1)
    scatter_hi(1, 0)
    scatter_down(1, 0)
    scatter_up(0, 1)
    scatter_hi(0, 0)
    scatter_down(0, 0)
    scatter_lo(0, 0)
    out[...] = sum_own().astype(BF16)

    for copy in started:
        copy.wait_send()


SENDS = 112


def local(*args):
    args = list(args)
    args[1] = args[1].reshape(1, COLS)
    anywhere = pl.BlockSpec(memory_space=pl.ANY)
    vm = pltpu.VMEM
    return pl.pallas_call(
        kernel,
        out_shape=jax.ShapeDtypeStruct((ROWS, COLS), BF16),
        in_specs=[anywhere] * 11 + [pl.BlockSpec(memory_space=pltpu.SMEM)],
        out_specs=pl.BlockSpec(memory_space=pltpu.VMEM),
        scratch_shapes=[
            vm((8, 8192), BF16),
            vm((1, COLS), F32),
            vm((2048, HID), BF16),
            vm((2048, HID), BF16),
            vm((HID, COLS), BF16),
            vm((128, COLS), BF16),
            vm((2, 8192), BF16),
            vm((2, HEAD_DIM), BF16),
            vm((2, HEAD_DIM), BF16),
            vm((2, 2048, HEAD_DIM), BF16),
            vm((2, 2048, HEAD_DIM), BF16),
            vm((2, HEADS, HEAD_DIM), F32),
            vm((2, 2, NX, 4, ROWS, COLS), BF16),
            vm((2, 2, 2, 2, 64, HID), BF16),
            vm((2, 2, 2, 64, HID), BF16),
            vm((2, 2, 2, 64, HID), BF16),
            vm((2, 2, 2, 64, HID), BF16),
            vm((2, 2, 2, 64, HID), BF16),
            vm((4, 2, HEADS, HEAD_DIM), BF16),
            vm((2, HEADS, 8, 128), F32),
            vm((NZ, NX, 2, 8, 128), BF16),
            vm((NX, NZ, 2, 8, 128), BF16),
            vm((NX, NZ, 2, 8, 128), BF16),
            vm((NX, NZ, 8, 128), BF16),
            vm((2, 2, NX, 4, ROWS, COLS), BF16),
            vm((2, 2, 2, 2, ROWS, COLS), BF16),
            vm((2, 2, 2, 2, ROWS, COLS), BF16),
            vm((2, 2, 2, 2, ROWS, COLS), BF16),
            vm((2, 2, 4, ROWS, COLS), BF16),
            vm((2, 5, ROWS, COLS), BF16),
            vm((2, 2, ROWS, COLS), BF16),
            vm((2, 2, ROWS, COLS), BF16),
            pltpu.SemaphoreType.DMA((11,)),
            pltpu.SemaphoreType.DMA((SENDS,)),
            pltpu.SemaphoreType.DMA((SENDS,)),
        ],
        compiler_params=pltpu.CompilerParams(
            collective_id=0, has_side_effects=True, vmem_limit_bytes=56 * 1024 * 1024
        ),
    )(*args)


def solution(mesh):
    return jax.shard_map(
        local,
        mesh=mesh,
        in_specs=(
            P("wide", None),
            P("narrow"),
            P("narrow", "wide"),
            P("narrow", "wide"),
            P("wide", "narrow"),
            P("wide", "narrow"),
            P(("wide", "narrow"), None),
            P(("wide", "narrow"), None),
            P(("wide", "narrow"), None),
            P(("wide", "narrow"), None, None),
            P(("wide", "narrow"), None, None),
            P(("wide", "narrow")),
        ),
        out_specs=P("wide", "narrow"),
        check_vma=False,
    )
```
